256 devices in a mesh: dp: 4 (over x_lo, core), wide: 16 (over x_hi, z), narrow: 4 (over y).
Axes of the slice: x: 4 (x_hi: 2, x_lo: 2; x = x_hi * 2 + x_lo), y: 4, z: 8, core: 2. Of those that a mesh axis runs over, the one named last changes fastest.
Arguments:
- tokens: bfloat16 [8192, 4096], P(('wide', 'narrow')), may hold values from -6 to 6
- grads_out: bfloat16 [8192, 4096], P(('wide', 'narrow')), may hold values from -1.5 to 1.5
- expert_ids: int32 [8192, 2], P(('wide', 'narrow')), may hold values from 0 to 63, all different within a row; in each aligned block of 128 rows (0 to 127, 128 to 255, ...) at most 8 rows name the same one
- gates: float32 [8192, 2], P(('wide', 'narrow')), may hold values from 0.1 to 1
- w_gate: bfloat16 [64, 768, 4096], P(('wide', 'narrow'), 'dp'), may hold values from -0.09375 to 0.09375
- w_up: bfloat16 [64, 768, 4096], P(('wide', 'narrow'), 'dp'), may hold values from -0.09375 to 0.09375
- w_down: bfloat16 [64, 768, 4096], P(('wide', 'narrow'), 'dp'), may hold values from -0.21875 to 0.21875
Outputs:
- input_grad: bfloat16 [8192, 4096], P(('wide', 'narrow'), 'dp')
- gate_grad: float32 [8192, 2], P(('wide', 'narrow'))
- grad_gate: bfloat16 [64, 768, 4096], P(('wide', 'narrow'), 'dp')
- grad_up: bfloat16 [64, 768, 4096], P(('wide', 'narrow'), 'dp')
- grad_down: bfloat16 [64, 768, 4096], P(('wide', 'narrow'), 'dp')
The draws below stay inside these ranges and needn't reach their ends.
Inputs may be any that keep to these rules, and one draw needn't show every extreme that they name: `expert_ids`: each token names 2 different experts. Among the 128 tokens of one group no expert is named by more than 8 tokens, a bound that some of them reach.
All inputs are finite; a program needn't handle non-finite values.
Results may differ from the reference program's by a relative error of at most 0.0075.
Values may be sent and summed in bfloat16 or wider, within the bound.
No kernel may reach another device: no remote copies, remote signals or barrier semaphores. Data moves between devices by JAX's collectives and lax.ppermute only.
A program may use at most 128 MiB of HBM per device.

```python
import math
import jax
import jax.numpy as jnp
import numpy as np
from jax import lax

D = 4096
FF = 768
TOP = 2
TOK_DEV = 128
EXPERTS = 64
TOKENS = 8192
C_SEND = 8


def level_of(stream_key, extent, split, smallest, high):
    level, own = 1.0, jax.random.fold_in(stream_key, 6)
    for axis_at, parts in split:
        heights = jnp.exp(jax.random.uniform(jax.random.fold_in(own, axis_at), (parts,), jnp.float32, smallest / len(split), high / len(split)))
        level = level * jnp.repeat(heights, extent[axis_at] // parts).reshape([-1 if axis == axis_at else 1 for axis in range(len(extent))])
    return level


def deal_out(rng, own, number, rows, number_of, top, limit, slope):
    ranking = jax.random.permutation(rng, number_of)
    packed, usual = load_shares(number_of, rows * top, limit, slope, True), load_shares(number_of, rows * top, limit, slope, False)
    places = jnp.arange(number_of)

    def named(sizes, turn):
        used = int((sizes > 0).sum())
        fixed = max(1, used // 4)
        passed = fixed + (places - fixed + turn * (used - fixed)) % max(1, number_of - fixed)
        return jnp.zeros((number_of,), jnp.int32).at[ranking[jnp.where(places < fixed, places, passed)]].set(jnp.asarray(sizes, jnp.int32))

    sizes = jnp.where(number % 4 == 0, named(packed, number // 4), named(usual, number - number // 4 - 1))
    mixed = jax.random.permutation(jax.random.fold_in(own, 3), number_of)
    donor, taker = mixed[0:number_of // 2 * 2:2], mixed[1:number_of // 2 * 2:2]
    margin = jnp.minimum(sizes[donor] - 1, limit - sizes[taker]) // 2
    margin = jnp.where((donor == ranking[0]) | (taker == ranking[0]) | (sizes[taker] == 0), 0, jnp.maximum(margin, 0))
    passed = jax.random.randint(jax.random.fold_in(own, 4), (number_of // 2,), 0, 1 << 20) % (margin + 1)
    sizes = sizes.at[donor].add(-passed).at[taker].add(passed)
    labels = jnp.searchsorted(jnp.cumsum(sizes), jnp.arange(rows * top), side="right").astype(jnp.int32)
    table = labels.reshape(top, rows).T
    table = table[jax.random.permutation(jax.random.fold_in(own, 1), rows)]
    turn = jax.random.randint(jax.random.fold_in(own, 2), (rows, 1), 0, top)
    return jnp.take_along_axis(table, (jnp.arange(top)[None, :] + turn) % top, axis=1)


def load_shares(count, total, limit, slope, full):
    weights = [(1 << 20) // math.isqrt(grade ** slope) + 1 for grade in range(1, count + 1)]
    largest = limit if full else min(limit, max(-(-total // count), total * weights[0] // sum(weights)))
    least = 1 if total - largest >= count - 1 else 0
    given, rest = [largest] + [least] * (count - 1), total - largest - least * (count - 1)
    while rest > 0:
        candidates = [i for i in range(1, count) if given[i] < largest] or [i for i in range(1, count) if given[i] < limit]
        pool, budget = sum([weights[i] for i in candidates]), rest
        for i in candidates:
            extra = min(limit - given[i], max(1, budget * weights[i] // pool), rest)
            given[i] = given[i] + extra
            rest = rest - extra
    return np.array(given)


def gaussian(key, dims, deviation, reach, cuts=(), held_as=jnp.bfloat16):
    values = deviation * jax.random.normal(key, dims, jnp.float32)
    if cuts:
        values = values * level_of(key, dims, cuts, -0.22, 0.18)
    return jnp.clip(values, -reach, reach).astype(held_as)


def setup_inputs(seed: int = 0) -> dict:
    arg_keys = jax.random.split(jax.random.key(seed), 8)
    tokens = gaussian(arg_keys[0], (TOKENS, D), 1.0, 6.0, ((0, 64),))
    grads_out = gaussian(arg_keys[1], (TOKENS, D), 0.25, 1.5, ((0, 64),))
    expert_ids_keys = jax.random.split(jax.random.fold_in(arg_keys[2], 1), TOKENS // TOK_DEV)
    expert_ids_turns = jax.random.permutation(jax.random.fold_in(arg_keys[2], 3), TOKENS // TOK_DEV)
    expert_ids = jax.vmap(lambda own, number: deal_out(jax.random.fold_in(arg_keys[2], 2), own, number, TOK_DEV, EXPERTS, TOP, C_SEND, 2))(expert_ids_keys, expert_ids_turns).reshape((TOKENS, TOP))
    gates = jnp.clip(jnp.exp(math.log(1.0) - 2.3025851 * jax.random.uniform(arg_keys[3], (TOKENS, TOP), jnp.float32) ** level_of(arg_keys[3], (TOKENS, TOP), ((0, 64),), -0.2, 0.2)), 0.1, 1.0)
    w_gate = gaussian(arg_keys[4], (EXPERTS, FF, D), D ** -0.5, 0.09375, ((0, 64), (1, 4)))
    w_up = gaussian(arg_keys[5], (EXPERTS, FF, D), D ** -0.5, 0.09375, ((0, 64), (1, 4)))
    w_down = gaussian(arg_keys[6], (EXPERTS, FF, D), FF ** -0.5, 0.21875, ((0, 64), (1, 4)))
    return dict(tokens=tokens, grads_out=grads_out, expert_ids=expert_ids, gates=gates, w_gate=w_gate, w_up=w_up, w_down=w_down)


def silu_grad(values):
    sig = jax.nn.sigmoid(values)
    return sig * (1.0 + values * (1.0 - sig))

def reference(tokens, grads_out, expert_ids, gates, w_gate, w_up, w_down):
    senders = TOKENS // TOK_DEV
    blocks = expert_ids.reshape(senders, TOK_DEV * TOP)
    onehot = (blocks[:, :, None] == jnp.arange(EXPERTS, dtype=jnp.int32)[None, None, :]).astype(jnp.int32)
    earlier = jnp.cumsum(onehot, axis=1) - onehot
    slot_pos = lax.optimization_barrier(jnp.sum(earlier * onehot, axis=2)).astype(jnp.int32)
    flat_rows = jnp.arange(TOKENS * TOP, dtype=jnp.int32).reshape(senders, TOK_DEV * TOP)
    sender = jnp.broadcast_to(jnp.arange(senders, dtype=jnp.int32)[:, None], blocks.shape)
    slot_table = jnp.zeros((EXPERTS, senders, C_SEND), jnp.int32).at[blocks, sender, slot_pos].set(flat_rows + 1)
    slot_table = slot_table.reshape(EXPERTS, senders * C_SEND)
    gate_flat = gates.reshape(-1)

    def expert_step(state_pair, inputs):
        input_sum, dgate_sum = state_pair
        index_list, gate_mat, up_mat, down_mat = inputs
        is_valid = index_list > 0
        flat_row = jnp.maximum(index_list - 1, 0).astype(jnp.int32)
        token_index = (flat_row // TOP).astype(jnp.int32)
        token_rows = jnp.where(is_valid[:, None], tokens[token_index], jnp.zeros((), tokens.dtype))
        grad_rows = jnp.where(is_valid[:, None], grads_out[token_index], jnp.zeros((), grads_out.dtype))
        gate_pre = jnp.dot(token_rows, gate_mat.T, preferred_element_type=jnp.float32)
        up_pre = jnp.dot(token_rows, up_mat.T, preferred_element_type=jnp.float32)
        activated = jax.nn.silu(gate_pre)
        hidden = (activated * up_pre).astype(jnp.bfloat16)
        hidden_grad = jnp.dot(grad_rows, down_mat.T, preferred_element_type=jnp.float32)
        gate_dot = lax.optimization_barrier(jnp.sum(hidden.astype(jnp.float32) * hidden_grad, axis=1))
        up_grad = (hidden_grad * activated).astype(jnp.bfloat16)
        pre_grad = (hidden_grad * up_pre * silu_grad(gate_pre)).astype(jnp.bfloat16)
        grad_down = jnp.dot(hidden.T, grad_rows, preferred_element_type=jnp.float32).astype(jnp.bfloat16)
        grad_gate = jnp.dot(pre_grad.T, token_rows, preferred_element_type=jnp.float32).astype(jnp.bfloat16)
        grad_up = jnp.dot(up_grad.T, token_rows, preferred_element_type=jnp.float32).astype(jnp.bfloat16)
        row_grad = jnp.dot(pre_grad, gate_mat, preferred_element_type=jnp.float32)
        row_grad = row_grad + jnp.dot(up_grad, up_mat, preferred_element_type=jnp.float32)
        weight = jnp.where(is_valid, gate_flat[flat_row], jnp.zeros((), jnp.float32))
        input_sum = input_sum.at[token_index].add(weight[:, None] * row_grad)
        dgate_sum = dgate_sum.at[flat_row].add(jnp.where(is_valid, gate_dot, jnp.zeros((), jnp.float32)))
        return ((input_sum, dgate_sum), (grad_gate, grad_up, grad_down))
    start_state = (jnp.zeros((TOKENS, D), jnp.float32), jnp.zeros((TOKENS * TOP,), jnp.float32))
    (input_sum, dgate_sum), (grad_gate, grad_up, grad_down) = lax.scan(expert_step, start_state, (slot_table, w_gate, w_up, w_down))
    return (input_sum.astype(jnp.bfloat16), dgate_sum.reshape(TOKENS, TOP), grad_gate, grad_up, grad_down)
```

```python
import functools

import jax
import jax.numpy as jnp
from jax import lax
from jax.experimental import pallas as pl
from jax.experimental.pallas import tpu as pltpu
from jax.sharding import Mesh, PartitionSpec as P

F32 = jnp.float32
BF16 = jnp.bfloat16
LANES = 128
VMEM_LIMIT = 56 * 1024 * 1024
ROWS = ("xhi", "z", "y")
PARTS = ("xlo", "core")


def silu_grad(values):
    sig = jax.nn.sigmoid(values)
    return sig * (1.0 + values * (1.0 - sig))


def dot(a, b, dims):
    return lax.dot_general(a, b, (dims, ((), ())), preferred_element_type=F32)


NN = ((1,), (0,))
NT = ((1,), (1,))
TN = ((0,), (0,))


def three_parts(value):
    high = value.astype(BF16)
    rest = value - high.astype(F32)
    middle = rest.astype(BF16)
    return high, middle, (rest - middle.astype(F32)).astype(BF16)


def in_lanes(parts, rows):
    lane = lax.broadcasted_iota(jnp.int32, (rows, LANES), 1)
    block = jnp.zeros((rows, LANES), F32)
    for i, part in enumerate(parts):
        block = jnp.where(lane == i, part.astype(F32), block)
    return block.astype(BF16)


def call(kernel, outs, args, flops, smem=0):
    moved = sum(a.size * a.dtype.itemsize for a in args) + sum(
        int(jnp.dtype(t).itemsize) * functools.reduce(lambda x, y: x * y, s, 1) for s, t in outs
    )
    vmem = pl.BlockSpec(memory_space=pltpu.VMEM)
    result = pl.pallas_call(
        kernel,
        out_shape=[jax.ShapeDtypeStruct(s, t) for s, t in outs],
        in_specs=[vmem] * len(args),
        out_specs=[vmem] * len(outs),
        compiler_params=pltpu.CompilerParams(vmem_limit_bytes=VMEM_LIMIT),
        cost_estimate=pl.CostEstimate(flops=flops, bytes_accessed=moved, transcendentals=0),
    )(*args)
    return result


def columns(start_block, width):
    return pl.ds(pl.multiple_of(start_block * width, LANES), width)


def place_tokens(capacity, ids_ref, tokens_ref, sent_ref, first_ref, second_ref):
    slots, quarter = sent_ref.shape
    rows = ids_ref.shape[1]
    slot = lax.broadcasted_iota(jnp.int32, (slots, rows), 0)
    expert = slot // capacity
    first = expert == ids_ref[0:1, :]
    second = expert == ids_ref[1:2, :]
    named = jnp.where(first | second, 1.0, 0.0)
    before = lax.broadcasted_iota(jnp.int32, (rows, rows), 0) < lax.broadcasted_iota(
        jnp.int32, (rows, rows), 1
    )
    earlier = dot(named.astype(BF16), jnp.where(before, 1.0, 0.0).astype(BF16), NN)
    here = earlier == (slot % capacity).astype(F32)
    first_ref[...] = jnp.where(first & here, 1.0, 0.0).astype(BF16)
    second_ref[...] = jnp.where(second & here, 1.0, 0.0).astype(BF16)
    placing = jnp.where((first | second) & here, 1.0, 0.0).astype(BF16)
    mine = lax.axis_index("xlo") * 2 + lax.axis_index("core")
    sent_ref[...] = dot(placing, tokens_ref[:, columns(mine, quarter)], NN).astype(BF16)


def place_grads(first_ref, second_ref, grads_ref, sent_ref):
    half = sent_ref.shape[1]
    placing = first_ref[...] + second_ref[...]
    mine = lax.axis_index("core")
    sent_ref[...] = dot(placing, grads_ref[:, columns(mine, half)], NN).astype(BF16)


def quarters():
    xlo, core = lax.axis_index("xlo"), lax.axis_index("core")
    return (xlo * 2 + core, (1 - xlo) * 2 + core, xlo * 2 + 1 - core, (1 - xlo) * 2 + 1 - core)


def forward(x0, x1, x2, x3, gate_ref, up_ref, act_ref, pre_ref, hidden_ref):
    quarter = x0.shape[1]
    gate_pre = jnp.zeros(act_ref.shape, F32)
    up_pre = jnp.zeros(act_ref.shape, F32)
    for piece, at in zip((x0, x1, x2, x3), quarters()):
        rows = piece[...]
        gate_pre += dot(rows, gate_ref[0, :, columns(at, quarter)], NT)
        up_pre += dot(rows, up_ref[0, :, columns(at, quarter)], NT)
    activated = gate_pre * jax.nn.sigmoid(gate_pre)
    act_ref[...] = activated
    pre_ref[...] = up_pre * silu_grad(gate_pre)
    hidden_ref[...] = (activated * up_pre).astype(BF16)


def own_hidden_grad(grads_ref, down_ref, out_ref):
    half = grads_ref.shape[1]
    at = lax.axis_index("core")
    out_ref[...] = dot(grads_ref[...], down_ref[0, :, columns(at, half)], NT)


def cotangents(
    own_ref, grads_ref, down_ref, act_ref, pre_ref, hidden_ref, gate_ref, up_ref,
    pre_grad_ref, up_grad_ref, dot_ref, sent_ref,
):
    rows, half = grads_ref.shape
    other = 1 - lax.axis_index("core")
    hidden_grad = own_ref[...] + dot(grads_ref[...], down_ref[0, :, columns(other, half)], NT)
    pre_grad = (hidden_grad * pre_ref[...]).astype(BF16)
    up_grad = (hidden_grad * act_ref[...]).astype(BF16)
    pre_grad_ref[...] = pre_grad
    up_grad_ref[...] = up_grad
    gate_dot = jnp.sum(hidden_ref[...].astype(F32) * hidden_grad, axis=1, keepdims=True)
    dot_ref[...] = jnp.broadcast_to(gate_dot, dot_ref.shape)
    quarter = half // 2
    for i in range(2):
        at = columns(2 * i + other, quarter)
        row_grad = dot(pre_grad, gate_ref[0, :, at], NN) + dot(up_grad, up_ref[0, :, at], NN)
        sent_ref[:, i * quarter : (i + 1) * quarter] = row_grad.astype(BF16)
    sent_ref[:, half:] = in_lanes(three_parts(gate_dot), rows)


def lane_sum(block, start, count):
    lane = lax.broadcasted_iota(jnp.int32, block.shape, 1)
    inside = (lane >= start) & (lane < start + count)
    return jnp.sum(jnp.where(inside, block, 0.0), axis=1, keepdims=True)


def chip_row_grad(pre_grad_ref, up_grad_ref, dot_ref, got_ref, gate_ref, up_ref, out_ref):
    rows, half = out_ref.shape[0], out_ref.shape[1] - LANES
    quarter = half // 2
    pre_grad, up_grad = pre_grad_ref[...], up_grad_ref[...]
    for i in range(2):
        at = columns(2 * i + lax.axis_index("core"), quarter)
        here = slice(i * quarter, (i + 1) * quarter)
        row_grad = dot(pre_grad, gate_ref[0, :, at], NN) + dot(up_grad, up_ref[0, :, at], NN)
        out_ref[:, here] = (row_grad + got_ref[:, here].astype(F32)).astype(BF16)
    gate_dot = dot_ref[:, 0:1] + lane_sum(got_ref[:, half:].astype(F32), 0, 3)
    out_ref[:, half:] = in_lanes(three_parts(gate_dot), rows)


def weight_grads_down(hidden_ref, g0, g1, out_ref):
    half = g0.shape[1]
    at = lax.axis_index("core")
    hidden = hidden_ref[...]
    out_ref[0, :, columns(at, half)] = dot(hidden, g0[...], TN).astype(BF16)
    out_ref[0, :, columns(1 - at, half)] = dot(hidden, g1[...], TN).astype(BF16)


def weight_grads(pre_grad_ref, up_grad_ref, x0, x1, x2, x3, gate_out, up_out):
    quarter = x0.shape[1]
    pre_grad, up_grad = pre_grad_ref[...], up_grad_ref[...]
    for piece, at in zip((x0, x1, x2, x3), quarters()):
        rows = piece[...]
        gate_out[0, :, columns(at, quarter)] = dot(pre_grad, rows, TN).astype(BF16)
        up_out[0, :, columns(at, quarter)] = dot(up_grad, rows, TN).astype(BF16)


def combine(first_ref, second_ref, back_ref, gates_ref, keep_ref, dots_ref, sent_ref):
    rows, quarter = keep_ref.shape
    half = 2 * quarter
    xlo = lax.axis_index("xlo")
    sums = []
    for at in (xlo, 1 - xlo):
        block = back_ref[:, columns(at, quarter)]
        total = gates_ref[:, 0:1] * dot(first_ref[...], block, TN)
        sums.append(total + gates_ref[:, 1:2] * dot(second_ref[...], block, TN))
    keep_ref[...] = sums[0]
    sent_ref[:, :quarter] = sums[1].astype(BF16)
    tail = back_ref[:, half:]
    dots = [lane_sum(dot(which[...], tail, TN), 0, 3) for which in (first_ref, second_ref)]
    lane = lax.broadcasted_iota(jnp.int32, dots_ref.shape, 1)
    dots_ref[...] = jnp.where(lane == 0, dots[0], dots[1])
    sent_ref[:, quarter:] = in_lanes(three_parts(dots[0]) + three_parts(dots[1]), rows)


def finish(keep_ref, dots_ref, got_ref, out_ref, gate_ref):
    quarter = keep_ref.shape[1]
    out_ref[...] = (keep_ref[...] + got_ref[:, :quarter].astype(F32)).astype(BF16)
    tail = got_ref[:, quarter:].astype(F32)
    lane = lax.broadcasted_iota(jnp.int32, gate_ref.shape, 1)
    got = jnp.where(lane == 0, lane_sum(tail, 0, 3), lane_sum(tail, 3, 3))
    gate_ref[...] = dots_ref[...] + got


def body(tokens, grads_out, expert_ids, gates, w_gate, w_up, w_down):
    rows, width = tokens.shape
    hidden_units = w_gate.shape[1]
    experts = lax.axis_size("xhi") * lax.axis_size("z") * lax.axis_size("y")
    capacity = 8
    slots = experts * capacity
    half, quarter = width // 2, width // 4
    swap = [(0, 1), (1, 0)]

    def exchange(value, axis):
        return lax.ppermute(value, axis, swap)

    def to_experts(value):
        shaped = value.reshape(experts, capacity, value.shape[1])
        return lax.all_to_all(shaped, ROWS, split_axis=0, concat_axis=0, tiled=True).reshape(
            value.shape
        )

    unit = 2 * slots * hidden_units * quarter
    sent_x, first, second = call(
        functools.partial(place_tokens, capacity),
        [((slots, quarter), BF16), ((slots, rows), BF16), ((slots, rows), BF16)],
        [expert_ids.T, tokens],
        2 * slots * rows * quarter,
    )
    x0 = to_experts(sent_x)
    (sent_g,) = call(
        place_grads, [((slots, half), BF16)], [first, second, grads_out], 2 * slots * rows * half
    )
    x0, sent_g = lax.optimization_barrier((x0, sent_g))
    g0 = to_experts(sent_g)
    x1 = exchange(x0, "xlo")
    x2 = exchange(x0, "core")
    x3 = exchange(x1, "core")
    act, pre, hidden = call(
        forward,
        [((slots, hidden_units), F32), ((slots, hidden_units), F32), ((slots, hidden_units), BF16)],
        [x0, x1, x2, x3, w_gate, w_up],
        8 * unit,
    )
    act, pre, hidden, g0 = lax.optimization_barrier((act, pre, hidden, g0))
    g1 = exchange(g0, "core")
    (own,) = call(own_hidden_grad, [((slots, hidden_units), F32)], [g0, w_down], 2 * unit)
    pre_grad, up_grad, dots, sent_r = call(
        cotangents,
        [
            ((slots, hidden_units), BF16),
            ((slots, hidden_units), BF16),
            ((slots, LANES), F32),
            ((slots, half + LANES), BF16),
        ],
        [own, g1, w_down, act, pre, hidden, w_gate, w_up],
        6 * unit,
    )
    got_r = exchange(sent_r, "core")
    (row_grad,) = call(
        chip_row_grad,
        [((slots, half + LANES), BF16)],
        [pre_grad, up_grad, dots, got_r, w_gate, w_up],
        4 * unit,
    )
    row_grad, pre_grad, up_grad, hidden = lax.optimization_barrier(
        (row_grad, pre_grad, up_grad, hidden)
    )
    back = to_experts(row_grad)
    (grad_down,) = call(weight_grads_down, [(w_down.shape, BF16)], [hidden, g0, g1], 4 * unit)
    grad_gate, grad_up = call(
        weight_grads,
        [(w_gate.shape, BF16), (w_up.shape, BF16)],
        [pre_grad, up_grad, x0, x1, x2, x3],
        8 * unit,
    )
    keep, token_dots, sent_t = call(
        combine,
        [((rows, quarter), F32), ((rows, 2), F32), ((rows, quarter + LANES), BF16)],
        [first, second, back, gates],
        4 * slots * rows * half,
    )
    got_t = exchange(sent_t, "xlo")
    input_grad, gate_grad = call(
        finish, [((rows, quarter), BF16), ((rows, 2), F32)], [keep, token_dots, got_t], rows * half
    )
    return input_grad, gate_grad, grad_gate, grad_up, grad_down


def solution(mesh):
    dp, wide, narrow = (mesh.shape[name] for name in ("dp", "wide", "narrow"))
    fine = Mesh(
        mesh.devices.reshape(2, dp // 2, 2, wide // 2, narrow), ("xlo", "core", "xhi", "z", "y")
    )
    in_specs = (
        P(ROWS, None),
        P(ROWS, None),
        P(ROWS, None),
        P(ROWS, None),
        P(ROWS, PARTS, None),
        P(ROWS, PARTS, None),
        P(ROWS, PARTS, None),
    )
    out_specs = (
        P(ROWS, PARTS),
        P(ROWS, None),
        P(ROWS, PARTS, None),
        P(ROWS, PARTS, None),
        P(ROWS, PARTS, None),
    )
    return jax.shard_map(body, mesh=fine, in_specs=in_specs, out_specs=out_specs, check_vma=False)
```

```python
import itertools
import math

import jax
import jax.numpy as jnp
from jax import lax
from jax.experimental import pallas as pl
from jax.experimental.pallas import tpu as pltpu
from jax.sharding import Mesh, PartitionSpec as P

F32 = jnp.float32
BF16 = jnp.bfloat16
LANES = 128
TAIL = 16
CAPACITY = 8
MIB = 1024 * 1024
VMEM_LIMIT = 60 * MIB
ROWS = ("xhi", "z", "y")
PARTS = ("xlo", "core")
ALL = PARTS + ROWS
NN = ((1,), (0,))
NT = ((1,), (1,))
TN = ((0,), (0,))


def dot(a, b, dims):
    return lax.dot_general(a, b, (dims, ((), ())), preferred_element_type=F32)


def three_parts(value):
    high = value.astype(BF16).astype(F32)
    rest = value - high
    middle = rest.astype(BF16).astype(F32)
    return high, middle, (rest - middle).astype(BF16).astype(F32)


def in_rows(parts, height):
    row = lax.broadcasted_iota(jnp.int32, (height, parts[0].shape[1]), 0)
    block = jnp.zeros(row.shape, F32)
    for i, part in enumerate(parts):
        block = jnp.where(row == i, part, block)
    return block


class Copies:
    def __init__(self, sems):
        self.sems, self.used = sems, 0

    def start(self, source, target):
        copy = pltpu.make_async_copy(source, target, self.sems.at[self.used])
        self.used += 1
        copy.start()
        return copy


def call(kernel, outs, args, scratch, copies, flops, vmem=VMEM_LIMIT):
    moved = sum(a.size * a.dtype.itemsize for a in args)
    moved += sum(math.prod(s) * jnp.dtype(t).itemsize for s, t in outs)
    place = pl.BlockSpec(memory_space=pl.ANY)
    return pl.pallas_call(
        kernel,
        out_shape=[jax.ShapeDtypeStruct(s, t) for s, t in outs],
        in_specs=[place] * len(args),
        out_specs=[place] * len(outs),
        scratch_shapes=[pltpu.VMEM(s, t) for s, t in scratch] + [pltpu.SemaphoreType.DMA((copies,))],
        compiler_params=pltpu.CompilerParams(vmem_limit_bytes=vmem),
        cost_estimate=pl.CostEstimate(flops=flops, bytes_accessed=moved, transcendentals=0),
    )(*args)


def columns(block, width, start=0):
    return pl.ds(pl.multiple_of(start + block * width, LANES), width)


def xlo():
    return lax.axis_index("xlo")


def core():
    return lax.axis_index("core")


def side():
    return lax.bitwise_xor(lax.axis_index("xlo"), lax.axis_index("xhi"))


def piece_order():
    near, far, mine, other = side(), 1 - side(), core(), 1 - core()
    return (near * 2 + mine, far * 2 + mine, near * 2 + other, far * 2 + other)


def choices(ids, slots):
    rows = ids.shape[1]
    slot = lax.broadcasted_iota(jnp.int32, (slots, rows), 0)
    expert = slot // CAPACITY
    first, second = expert == ids[0:1, :], expert == ids[1:2, :]
    before = lax.broadcasted_iota(jnp.int32, (rows, rows), 0) < lax.broadcasted_iota(
        jnp.int32, (rows, rows), 1
    )
    named = jnp.where(first | second, 1.0, 0.0).astype(BF16)
    earlier = dot(named, jnp.where(before, 1.0, 0.0).astype(BF16), NN)
    here = earlier == (slot % CAPACITY).astype(F32)
    return jnp.where(first & here, 1.0, 0.0), jnp.where(second & here, 1.0, 0.0)


def write_parts(copies, placing, rows, sent, sent_hbm, start, stop, step):
    out = []
    for at in range(start, stop, step):
        part = slice(at, at + step)
        sent[:, part] = dot(placing, rows[:, at - start : at - start + step], NN).astype(BF16)
        out.append(copies.start(sent.at[:, part], sent_hbm.at[:, part]))
    return out


def place_first(ids_hbm, x_hbm, g_hbm, sent_hbm, ids, x, g, sent, sems):
    copies = Copies(sems)
    quarter, eighth = x.shape[1], g.shape[1]
    block = side() * 2 + core()
    got_ids = copies.start(ids_hbm, ids)
    got_x = copies.start(x_hbm.at[:, columns(block, quarter)], x)
    got_g = copies.start(g_hbm.at[:, columns(block, eighth)], g)
    got_ids.wait()
    first, second = choices(ids[...], sent.shape[0])
    placing = (first + second).astype(BF16)
    got_x.wait()
    out = write_parts(copies, placing, x, sent, sent_hbm, 0, quarter, eighth)
    got_g.wait()
    out += write_parts(copies, placing, g, sent, sent_hbm, quarter, quarter + eighth, eighth)
    for copy in out:
        copy.wait()


def place_second(ids_hbm, g_hbm, sent_hbm, ids, g, sent, sems):
    copies = Copies(sems)
    quarter = g.shape[1]
    got_ids = copies.start(ids_hbm, ids)
    got_g = copies.start(g_hbm.at[:, columns(core(), quarter, 2 * quarter)], g)
    got_ids.wait()
    first, second = choices(ids[...], sent.shape[0])
    placing = (first + second).astype(BF16)
    got_g.wait()
    for copy in write_parts(copies, placing, g, sent, sent_hbm, 0, quarter, quarter // 2):
        copy.wait()


def split(both_hbm, x_hbm, g_hbm, x, g, sems):
    copies = Copies(sems)
    parts = 4
    rows, width = x.shape[0] // parts, x.shape[1]
    got = []
    for held, at in ((x, pl.ds(0, width)), (g, pl.ds(width, g.shape[1]))):
        for i in range(parts):
            here = slice(i * rows, (i + 1) * rows)
            got.append(copies.start(both_hbm.at[here, at], held.at[here]))
    sent = []
    for j, (held, out) in enumerate(((x, x_hbm), (g, g_hbm))):
        for i in range(parts):
            here = slice(i * rows, (i + 1) * rows)
            got[j * parts + i].wait()
            sent.append(copies.start(held.at[here], out.at[here]))
    for copy in sent:
        copy.wait()


def pick(ids_hbm, first_hbm, second_hbm, ids, first, second, sems):
    copies = Copies(sems)
    copies.start(ids_hbm, ids).wait()
    values = choices(ids[...], first.shape[1])
    first[...] = jnp.transpose(values[0]).astype(BF16)
    second[...] = jnp.transpose(values[1]).astype(BF16)
    out = [copies.start(first, first_hbm), copies.start(second, second_hbm)]
    for copy in out:
        copy.wait()


def share_far(gate_hbm, up_hbm, far_both, both, sems):
    copies = Copies(sems)
    units, half = both.shape[0] // 2, both.shape[1]
    got = []
    for i, ref in enumerate((gate_hbm, up_hbm)):
        there = slice(i * units, (i + 1) * units)
        got.append(copies.start(ref.at[0, :, columns(1 - xlo(), half)], both.at[there]))
    sent = []
    for i in range(2):
        there = slice(i * units, (i + 1) * units)
        got[i].wait()
        sent.append(copies.start(both.at[there], far_both.at[there]))
    for copy in sent:
        copy.wait()


def share_near(gate_hbm, up_hbm, down_hbm, near_both, near_down, both, down, sems):
    copies = Copies(sems)
    units, quarter = both.shape[0] // 2, both.shape[1]
    eighth, other = quarter // 2, 1 - core()
    got = []
    for i, ref in enumerate((gate_hbm, up_hbm)):
        there = both.at[i * units : (i + 1) * units]
        got.append(copies.start(ref.at[0, :, columns(xlo() * 2 + other, quarter)], there))
    for i in range(2):
        there = down.at[:, i * eighth : (i + 1) * eighth]
        got.append(copies.start(down_hbm.at[0, :, columns(2 * i + other, eighth)], there))
    direct = down_hbm.at[0, :, columns(other, quarter, 2 * quarter)]
    got.append(copies.start(direct, down.at[:, quarter:]))
    for copy in got:
        copy.wait()
    sent = [copies.start(both, near_both), copies.start(down, near_down)]
    for copy in sent:
        copy.wait()


def pass_on(both_hbm, out_hbm, both, sems):
    copies = Copies(sems)
    copies.start(both_hbm.at[:, columns(1 - core(), both.shape[1])], both).wait()
    copies.start(both, out_hbm).wait()


def forward(x0, x1, x2, x3, gate_hbm, up_hbm, act_hbm, pre_hbm, hidden_hbm, *scratch):
    x, gate, up, act, pre, hidden, sems = scratch
    copies = Copies(sems)
    quarter = x.shape[2]
    started = []
    for i, (ref, at) in enumerate(zip((x0, x1, x2, x3), piece_order())):
        started.append(
            [
                copies.start(ref, x.at[i]),
                copies.start(gate_hbm.at[0, :, columns(at, quarter)], gate.at[i]),
                copies.start(up_hbm.at[0, :, columns(at, quarter)], up.at[i]),
            ]
        )
    gate_pre = jnp.zeros(act.shape, F32)
    up_pre = jnp.zeros(act.shape, F32)
    for i in range(4):
        for copy in started[i]:
            copy.wait()
        gate_pre += dot(gate[i], x[i], NT)
        up_pre += dot(up[i], x[i], NT)
    sig = jax.nn.sigmoid(gate_pre)
    activated = gate_pre * sig
    act[...] = activated
    pre[...] = up_pre * (sig * (1.0 + gate_pre * (1.0 - sig)))
    hidden[...] = (activated * up_pre).astype(BF16)
    out = [copies.start(a, b) for a, b in ((act, act_hbm), (pre, pre_hbm), (hidden, hidden_hbm))]
    for copy in out:
        copy.wait()


def hidden_grads(g0, g1, gd, down_hbm, near_hbm, mine_hbm, theirs_hbm, g, down, total, sems):
    copies = Copies(sems)
    units = down.shape[0] // 2
    quarter = g.shape[1] // 2
    eighth = quarter // 2
    parts = (slice(0, eighth), slice(eighth, quarter), slice(quarter, 2 * quarter))
    near, far = piece_order()[:2]
    own = (columns(near, eighth), columns(far, eighth), columns(core(), quarter, 2 * quarter))
    theirs = (columns(side(), eighth), columns(1 - side(), eighth), pl.ds(quarter, quarter))
    got = [
        [
            copies.start(ref, g.at[:, part]),
            copies.start(near_hbm.at[:, a], down.at[:units, part]),
            copies.start(down_hbm.at[0, :, b], down.at[units:, part]),
        ]
        for ref, part, a, b in zip((g0, g1, gd), parts, theirs, own)
    ]
    sums = jnp.zeros(total.shape, F32)
    for copy_list, part in zip(got, parts):
        for copy in copy_list:
            copy.wait()
        sums += dot(down[:, part], g[:, part], NT)
    total[...] = sums
    out = [copies.start(total.at[:units], theirs_hbm), copies.start(total.at[units:], mine_hbm)]
    for copy in out:
        copy.wait()


def cotangents(mine_hbm, got_hbm, act_hbm, pre_hbm, hidden_hbm, pack_hbm, *scratch):
    mine, got, act, pre, hidden, pack, sems = scratch
    copies = Copies(sems)
    units = mine.shape[0]
    pairs = ((mine_hbm, mine), (got_hbm, got), (pre_hbm, pre), (act_hbm, act), (hidden_hbm, hidden))
    started = [copies.start(a, b) for a, b in pairs]
    for copy in started:
        copy.wait()
    hidden_grad = mine[...] + got[...]
    pack[:units] = (hidden_grad * pre[...]).astype(BF16)
    pack[units : 2 * units] = (hidden_grad * act[...]).astype(BF16)
    gate_dot = jnp.sum(hidden[...].astype(F32) * hidden_grad, axis=0, keepdims=True)
    pack[2 * units :] = in_rows(three_parts(gate_dot), TAIL).astype(BF16)
    copies.start(pack, pack_hbm).wait()


def near_row_grad(own_hbm, near_hbm, gate_hbm, up_hbm, both_hbm, out_hbm, *scratch):
    own, near, mine, both, total, sems = scratch
    copies = Copies(sems)
    units, quarter = mine.shape[0] // 2, mine.shape[1]
    at = columns(xlo() * 2 + core(), quarter)
    started = [
        copies.start(own_hbm, own),
        copies.start(gate_hbm.at[0, :, at], mine.at[:units]),
        copies.start(up_hbm.at[0, :, at], mine.at[units:]),
        copies.start(near_hbm, near),
        copies.start(both_hbm, both),
    ]
    for copy in started:
        copy.wait()
    total[...] = dot(own[: 2 * units], mine[...], TN) + dot(near[: 2 * units], both[...], TN)
    copies.start(total, out_hbm).wait()


def row_grad(
    begun_hbm, own_hbm, near_hbm, far_hbm, last_hbm, far_both, last_both, out_hbm, *scratch
):
    total, own, near, far, last, wide, lasting, sent, sems = scratch
    copies = Copies(sems)
    units2, quarter = wide.shape
    pairs = (
        (far_hbm, far),
        (far_both.at[:, columns(core(), quarter)], wide),
        (last_hbm, last),
        (last_both, lasting),
        (begun_hbm, total),
        (own_hbm.at[units2:], own),
        (near_hbm.at[units2:], near),
    )
    started = [copies.start(a, b) for a, b in pairs]
    started[0].wait()
    far_rows = jnp.transpose(far[:units2])
    started[1].wait()
    started[2].wait()
    last_rows = jnp.transpose(last[:units2])
    started[5].wait()
    started[6].wait()
    tails = own[...].astype(F32) + near[...].astype(F32)
    tails += far[units2:].astype(F32) + last[units2:].astype(F32)
    gate_dot = jnp.sum(tails, axis=0, keepdims=True)
    sent[:, quarter:] = jnp.transpose(in_rows(three_parts(gate_dot), LANES)).astype(BF16)
    started[3].wait()
    started[4].wait()
    out = []
    for i in range(2):
        part = slice(i * (quarter // 2), (i + 1) * (quarter // 2))
        sums = dot(far_rows, wide[:, part], NN) + dot(last_rows, lasting[:, part], NN)
        sent[:, part] = (total[:, part] + sums).astype(BF16)
        if i:
            part = slice(quarter // 2, quarter + LANES)
        out.append(copies.start(sent.at[:, part], out_hbm.at[:, part]))
    for copy in out:
        copy.wait()


def weight_grads(pack_hbm, x0, x1, x2, x3, gate_hbm, up_hbm, pack, x, out, sems):
    copies = Copies(sems)
    units, quarter = out.shape[1] // 2, x.shape[2]
    got = [copies.start(pack_hbm.at[: 2 * units], pack)]
    got += [copies.start(ref, x.at[i]) for i, ref in enumerate((x0, x1, x2, x3))]
    got[0].wait()
    sent = []
    for i, at in enumerate(piece_order()):
        got[i + 1].wait()
        out[i] = dot(pack[...], x[i], NN).astype(BF16)
        there = columns(at, quarter)
        sent.append(copies.start(out.at[i, :units], gate_hbm.at[0, :, there]))
        sent.append(copies.start(out.at[i, units:], up_hbm.at[0, :, there]))
    for copy in sent:
        copy.wait()


def weight_grads_down(hidden_hbm, g0, g1, g2, g3, gd0, gd1, down_hbm, *scratch):
    hidden, g, gd, out, direct, sems = scratch
    copies = Copies(sems)
    eighth = g.shape[2]
    got = [copies.start(hidden_hbm, hidden)]
    got += [copies.start(ref, g.at[i]) for i, ref in enumerate((g0, g1, g2, g3))]
    got += [copies.start(ref, gd.at[i]) for i, ref in enumerate((gd0, gd1))]
    got[0].wait()
    sent = []
    for i, at in enumerate(piece_order()):
        got[i + 1].wait()
        out[i] = dot(hidden[...], g[i], NN).astype(BF16)
        sent.append(copies.start(out.at[i], down_hbm.at[0, :, columns(at, eighth)]))
    for i, at in enumerate((core(), 1 - core())):
        got[i + 5].wait()
        direct[i] = dot(hidden[...], gd[i], NN).astype(BF16)
        there = columns(at, 2 * eighth, 4 * eighth)
        sent.append(copies.start(direct.at[i], down_hbm.at[0, :, there]))
    for copy in sent:
        copy.wait()


def combine(first_hbm, second_hbm, back_hbm, gates_hbm, out_hbm, dots_hbm, *scratch):
    first, second, back, gates, out, dots, sems = scratch
    copies = Copies(sems)
    rows, quarter = out.shape
    parts = (slice(0, quarter // 2), slice(quarter // 2, quarter + LANES))
    pairs = ((gates_hbm, gates), (first_hbm, first), (second_hbm, second))
    started = [copies.start(a, b) for a, b in pairs]
    got = [copies.start(back_hbm.at[:, part], back.at[:, part]) for part in parts]
    for copy in started:
        copy.wait()
    weights = jnp.transpose(in_rows((gates[0:1, :], gates[1:2, :]), LANES))
    sent = []
    for i, part in enumerate(parts):
        got[i].wait()
        picked = [dot(ref[...], back[:, part], NN) for ref in (first, second)]
        total = weights[:, 0:1] * picked[0] + weights[:, 1:2] * picked[1]
        there = slice(i * (quarter // 2), (i + 1) * (quarter // 2))
        out[:, there] = total[:, : quarter // 2].astype(BF16)
        sent.append(copies.start(out.at[:, there], out_hbm.at[:, there]))
    lane = lax.broadcasted_iota(jnp.int32, (rows, LANES), 1)
    for i in range(2):
        tail = jnp.transpose(jnp.where(lane < 3, picked[i][:, quarter // 2 :], 0.0))
        dots[i : i + 1, :] = jnp.sum(tail, axis=0, keepdims=True)
    sent.append(copies.start(dots, dots_hbm))
    for copy in sent:
        copy.wait()


def crossing_groups(sizes):
    xhi, z, y = sizes
    groups = []
    for start, one in itertools.product(range(2), range(2)):
        groups.append(
            [
                ((((start ^ h) * 2 + one) * xhi + h) * z + i) * y + j
                for h, i, j in itertools.product(range(xhi), range(z), range(y))
            ]
        )
    return groups


def body(tokens, grads_out, expert_ids, gates, w_gate, w_up, w_down):
    rows, width = tokens.shape
    units = w_gate.shape[1]
    sizes = tuple(lax.axis_size(name) for name in ROWS)
    experts = sizes[0] * sizes[1] * sizes[2]
    slots = experts * CAPACITY
    quarter, half = width // 4, width // 2
    groups = crossing_groups(sizes)

    def exchange(value, axis):
        return lax.ppermute(value, axis, [(0, 1), (1, 0)])

    def to_experts(value):
        shaped = value.reshape(experts, CAPACITY, value.shape[1])
        moved = lax.all_to_all(
            shaped, ALL, split_axis=0, concat_axis=0, tiled=True, axis_index_groups=groups
        )
        return moved.reshape(value.shape)

    def to_tokens(value):
        shaped = value.reshape(experts, CAPACITY, value.shape[1])
        moved = lax.all_to_all(shaped, ROWS, split_axis=0, concat_axis=0, tiled=True)
        return moved.reshape(value.shape)

    unit = 2 * slots * units * quarter
    eighth = width // 8
    ids, gates = expert_ids.T, gates.T
    piece, wide, tall = ((slots, quarter), BF16), ((units, slots), F32), ((2 * units, quarter), BF16)
    pack = ((2 * units + TAIL, slots), BF16)
    hidden_type = ((units, slots), BF16)
    half_down = ((units, half), BF16)
    id_type, chosen = ((2, rows), jnp.int32), ((rows, slots), BF16)

    (sent_first,) = call(
        place_first,
        [((slots, quarter + eighth), BF16)],
        [ids, tokens, grads_out],
        [
            id_type,
            ((rows, quarter), BF16),
            ((rows, eighth), BF16),
            ((slots, quarter + eighth), BF16),
        ],
        6,
        unit // 2,
    )
    got_first = to_experts(sent_first)
    shared = ((2 * units, half), BF16)
    (far_both,) = call(share_far, [shared], [w_gate, w_up], [shared], 4, 1000)
    far_both = exchange(far_both, "xlo")
    near_both, near_down = call(
        share_near, [tall, half_down], [w_gate, w_up, w_down], [tall, half_down], 7, 1000
    )
    near_both, near_down = exchange(near_both, "core"), exchange(near_down, "core")
    (sent_second,) = call(
        place_second,
        [piece],
        [ids, grads_out],
        [id_type, ((rows, quarter), BF16), piece],
        4,
        unit // 2,
    )
    first, second = call(pick, [chosen, chosen], [ids], [id_type, chosen, chosen], 3, unit // 4)
    got_first, sent_second, first, second, near_both, near_down, far_both = (
        lax.optimization_barrier(
            (got_first, sent_second, first, second, near_both, near_down, far_both)
        )
    )
    eighth_piece = ((slots, eighth), BF16)
    x0, g0 = call(
        split, [piece, eighth_piece], [got_first], [piece, eighth_piece], 16, 1000, 8 * MIB
    )
    gd0 = to_experts(sent_second)
    x1 = exchange(x0, "xlo")
    x1, g0 = lax.optimization_barrier((x1, g0))
    g1 = exchange(g0, "xlo")
    x2 = exchange(x0, "core")
    x3 = exchange(x1, "core")
    act, pre, hidden = call(
        forward,
        [wide, wide, hidden_type],
        [x0, x1, x2, x3, w_gate, w_up],
        [
            ((4, slots, quarter), BF16),
            ((4, units, quarter), BF16),
            ((4, units, quarter), BF16),
            wide,
            wide,
            hidden_type,
        ],
        15,
        8 * unit,
    )
    act, pre, hidden, gd0, g1 = lax.optimization_barrier((act, pre, hidden, gd0, g1))
    mine, theirs = call(
        hidden_grads,
        [wide, wide],
        [g0, g1, gd0, w_down, near_down],
        [((slots, half), BF16), ((2 * units, half), BF16), ((2 * units, slots), F32)],
        11,
        4 * unit,
    )
    theirs, far_both = lax.optimization_barrier((theirs, far_both))
    got = exchange(theirs, "core")
    (last_both,) = call(pass_on, [tall], [far_both], [tall], 2, 1000)
    last_both = exchange(last_both, "core")
    (own,) = call(
        cotangents,
        [pack],
        [mine, got, act, pre, hidden],
        [wide, wide, wide, wide, hidden_type, pack],
        6,
        10 * slots * units,
        8 * MIB,
    )
    far = exchange(own, "xlo")
    near = exchange(own, "core")
    total = ((slots, quarter), F32)
    (begun,) = call(
        near_row_grad,
        [total],
        [own, near, w_gate, w_up, near_both],
        [pack, pack, tall, tall, total],
        6,
        4 * unit,
    )
    far, begun, g0, g1, gd0, hidden, own = lax.optimization_barrier(
        (far, begun, g0, g1, gd0, hidden, own)
    )
    last = exchange(far, "core")
    tail = ((TAIL, slots), BF16)
    returned = ((slots, quarter + LANES), BF16)
    (sent_r,) = call(
        row_grad,
        [returned],
        [begun, own, near, far, last, far_both, last_both],
        [total, tail, tail, pack, pack, tall, tall, returned],
        9,
        4 * unit,
    )
    sent_r, own, hidden, g0, g1, gd0 = lax.optimization_barrier(
        (sent_r, own, hidden, g0, g1, gd0)
    )
    back = to_tokens(sent_r)
    g2, g3, gd1 = exchange(g0, "core"), exchange(g1, "core"), exchange(gd0, "core")
    grad_gate, grad_up = call(
        weight_grads,
        [(w_gate.shape, BF16), (w_up.shape, BF16)],
        [own, x0, x1, x2, x3],
        [((2 * units, slots), BF16), ((4, slots, quarter), BF16), ((4, 2 * units, quarter), BF16)],
        13,
        8 * unit,
    )
    (grad_down,) = call(
        weight_grads_down,
        [(w_down.shape, BF16)],
        [hidden, g0, g1, g2, g3, gd0, gd1],
        [
            hidden_type,
            ((4, slots, eighth), BF16),
            ((2, slots, quarter), BF16),
            ((4, units, eighth), BF16),
            ((2, units, quarter), BF16),
        ],
        13,
        4 * unit,
    )
    back, grad_gate, grad_up, grad_down = lax.optimization_barrier(
        (back, grad_gate, grad_up, grad_down)
    )
    input_grad, gate_grad = call(
        combine,
        [((rows, quarter), BF16), ((2, rows), F32)],
        [first, second, back, gates],
        [chosen, chosen, returned, ((2, rows), F32), ((rows, quarter), BF16), ((2, rows), F32)],
        8,
        unit,
        8 * MIB,
    )
    return input_grad, gate_grad.T, grad_gate, grad_up, grad_down


def solution(mesh):
    dp, wide, narrow = (mesh.shape[name] for name in ("dp", "wide", "narrow"))
    fine = Mesh(mesh.devices.reshape(2, dp // 2, 2, wide // 2, narrow), ALL)
    by_row, by_part = P(ROWS, None), P(ROWS, PARTS, None)
    return jax.shard_map(
        body,
        mesh=fine,
        in_specs=(by_row, by_row, by_row, by_row, by_part, by_part, by_part),
        out_specs=(P(ROWS, PARTS), by_row, by_part, by_part, by_part),
        check_vma=False,
    )
```

```python
import itertools
import math

import jax
import jax.numpy as jnp
from jax import lax
from jax.experimental import pallas as pl
from jax.experimental.pallas import tpu as pltpu
from jax.sharding import Mesh, PartitionSpec as P

F32 = jnp.float32
BF16 = jnp.bfloat16
LANES = 128
TAIL = 16
CAPACITY = 8
MIB = 1024 * 1024
VMEM_LIMIT = 60 * MIB
ROWS = ("xhi", "z", "y")
PARTS = ("xlo", "core")
ALL = PARTS + ROWS
NN = ((1,), (0,))
NT = ((1,), (1,))
TN = ((0,), (0,))


def dot(a, b, dims):
    return lax.dot_general(a, b, (dims, ((), ())), preferred_element_type=F32)


def three_parts(value):
    high = value.astype(BF16).astype(F32)
    rest = value - high
    middle = rest.astype(BF16).astype(F32)
    return high, middle, (rest - middle).astype(BF16).astype(F32)


def in_rows(parts, height):
    row = lax.broadcasted_iota(jnp.int32, (height, parts[0].shape[1]), 0)
    block = jnp.zeros(row.shape, F32)
    for i, part in enumerate(parts):
        block = jnp.where(row == i, part, block)
    return block


class Copies:
    def __init__(self, sems):
        self.sems, self.used = sems, 0

    def start(self, source, target):
        copy = pltpu.make_async_copy(source, target, self.sems.at[self.used])
        self.used += 1
        copy.start()
        return copy


def call(kernel, outs, args, scratch, copies, flops, vmem=VMEM_LIMIT):
    moved = sum(a.size * a.dtype.itemsize for a in args)
    moved += sum(math.prod(s) * jnp.dtype(t).itemsize for s, t in outs)
    place = pl.BlockSpec(memory_space=pl.ANY)
    return pl.pallas_call(
        kernel,
        out_shape=[jax.ShapeDtypeStruct(s, t) for s, t in outs],
        in_specs=[place] * len(args),
        out_specs=[place] * len(outs),
        scratch_shapes=[pltpu.VMEM(s, t) for s, t in scratch] + [pltpu.SemaphoreType.DMA((copies,))],
        compiler_params=pltpu.CompilerParams(vmem_limit_bytes=vmem),
        cost_estimate=pl.CostEstimate(flops=flops, bytes_accessed=moved, transcendentals=0),
    )(*args)


def columns(block, width, start=0):
    return pl.ds(pl.multiple_of(start + block * width, LANES), width)


def xlo():
    return lax.axis_index("xlo")


def core():
    return lax.axis_index("core")


def side():
    return lax.bitwise_xor(lax.axis_index("xlo"), lax.axis_index("xhi"))


def piece_order():
    near, far, mine, other = side(), 1 - side(), core(), 1 - core()
    return (near * 2 + mine, far * 2 + mine, near * 2 + other, far * 2 + other)


def choices(ids, slots):
    rows = ids.shape[1]
    slot = lax.broadcasted_iota(jnp.int32, (slots, rows), 0)
    expert = slot // CAPACITY
    first, second = expert == ids[0:1, :], expert == ids[1:2, :]
    before = lax.broadcasted_iota(jnp.int32, (rows, rows), 0) < lax.broadcasted_iota(
        jnp.int32, (rows, rows), 1
    )
    named = jnp.where(first | second, 1.0, 0.0).astype(BF16)
    earlier = dot(named, jnp.where(before, 1.0, 0.0).astype(BF16), NN)
    here = earlier == (slot % CAPACITY).astype(F32)
    return jnp.where(first & here, 1.0, 0.0), jnp.where(second & here, 1.0, 0.0)


def write_parts(copies, placing, rows, sent, sent_hbm, start, stop, step):
    out = []
    for at in range(start, stop, step):
        part = slice(at, at + step)
        sent[:, part] = dot(placing, rows[:, at - start : at - start + step], NN).astype(BF16)
        out.append(copies.start(sent.at[:, part], sent_hbm.at[:, part]))
    return out


def place_first(ids_hbm, x_hbm, g_hbm, sent_hbm, ids, x, g, sent, sems):
    copies = Copies(sems)
    quarter, eighth = x.shape[1], g.shape[1]
    block = side() * 2 + core()
    got_ids = copies.start(ids_hbm, ids)
    got_x = copies.start(x_hbm.at[:, columns(block, quarter)], x)
    got_g = copies.start(g_hbm.at[:, columns(block, eighth)], g)
    got_ids.wait()
    first, second = choices(ids[...], sent.shape[0])
    placing = (first + second).astype(BF16)
    got_x.wait()
    out = write_parts(copies, placing, x, sent, sent_hbm, 0, quarter, eighth)
    got_g.wait()
    out += write_parts(copies, placing, g, sent, sent_hbm, quarter, quarter + eighth, eighth)
    for copy in out:
        copy.wait()


def place_second(ids_hbm, g_hbm, sent_hbm, ids, g, sent, sems):
    copies = Copies(sems)
    quarter = g.shape[1]
    got_ids = copies.start(ids_hbm, ids)
    got_g = copies.start(g_hbm.at[:, columns(core(), quarter, 2 * quarter)], g)
    got_ids.wait()
    first, second = choices(ids[...], sent.shape[0])
    placing = (first + second).astype(BF16)
    got_g.wait()
    for copy in write_parts(copies, placing, g, sent, sent_hbm, 0, quarter, quarter // 2):
        copy.wait()


def split(both_hbm, x_hbm, g_hbm, x, g, sems):
    copies = Copies(sems)
    parts = 4
    rows, width = x.shape[0] // parts, x.shape[1]
    got = []
    for held, at in ((x, pl.ds(0, width)), (g, pl.ds(width, g.shape[1]))):
        for i in range(parts):
            here = slice(i * rows, (i + 1) * rows)
            got.append(copies.start(both_hbm.at[here, at], held.at[here]))
    sent = []
    for j, (held, out) in enumerate(((x, x_hbm), (g, g_hbm))):
        for i in range(parts):
            here = slice(i * rows, (i + 1) * rows)
            got[j * parts + i].wait()
            sent.append(copies.start(held.at[here], out.at[here]))
    for copy in sent:
        copy.wait()


def pick(ids_hbm, first_hbm, second_hbm, ids, first, second, sems):
    copies = Copies(sems)
    copies.start(ids_hbm, ids).wait()
    values = choices(ids[...], first.shape[1])
    first[...] = jnp.transpose(values[0]).astype(BF16)
    second[...] = jnp.transpose(values[1]).astype(BF16)
    out = [copies.start(first, first_hbm), copies.start(second, second_hbm)]
    for copy in out:
        copy.wait()


def share_far(gate_hbm, up_hbm, far_both, both, sems):
    copies = Copies(sems)
    units, half = both.shape[0] // 2, both.shape[1]
    got = []
    for i, ref in enumerate((gate_hbm, up_hbm)):
        there = slice(i * units, (i + 1) * units)
        got.append(copies.start(ref.at[0, :, columns(1 - xlo(), half)], both.at[there]))
    sent = []
    for i in range(2):
        there = slice(i * units, (i + 1) * units)
        got[i].wait()
        sent.append(copies.start(both.at[there], far_both.at[there]))
    for copy in sent:
        copy.wait()


def share_near(gate_hbm, up_hbm, down_hbm, near_both, near_down, both, down, sems):
    copies = Copies(sems)
    units, quarter = both.shape[0] // 2, both.shape[1]
    eighth, other = quarter // 2, 1 - core()
    got = []
    for i, ref in enumerate((gate_hbm, up_hbm)):
        there = both.at[i * units : (i + 1) * units]
        got.append(copies.start(ref.at[0, :, columns(xlo() * 2 + other, quarter)], there))
    for i in range(2):
        there = down.at[:, i * eighth : (i + 1) * eighth]
        got.append(copies.start(down_hbm.at[0, :, columns(2 * i + other, eighth)], there))
    direct = down_hbm.at[0, :, columns(other, quarter, 2 * quarter)]
    got.append(copies.start(direct, down.at[:, quarter:]))
    for copy in got:
        copy.wait()
    sent = [copies.start(both, near_both), copies.start(down, near_down)]
    for copy in sent:
        copy.wait()


def pass_on(both_hbm, out_hbm, both, sems):
    copies = Copies(sems)
    copies.start(both_hbm.at[:, columns(1 - core(), both.shape[1])], both).wait()
    copies.start(both, out_hbm).wait()


def forward(x0, x1, x2, x3, gate_hbm, up_hbm, act_hbm, pre_hbm, hidden_hbm, *scratch):
    x, gate, up, act, pre, hidden, sems = scratch
    copies = Copies(sems)
    quarter = x.shape[2]
    started = []
    for i, (ref, at) in enumerate(zip((x0, x1, x2, x3), piece_order())):
        started.append(
            [
                copies.start(ref, x.at[i]),
                copies.start(gate_hbm.at[0, :, columns(at, quarter)], gate.at[i]),
                copies.start(up_hbm.at[0, :, columns(at, quarter)], up.at[i]),
            ]
        )
    gate_pre = jnp.zeros(act.shape, F32)
    up_pre = jnp.zeros(act.shape, F32)
    for i in range(4):
        for copy in started[i]:
            copy.wait()
        gate_pre += dot(gate[i], x[i], NT)
        up_pre += dot(up[i], x[i], NT)
    sig = jax.nn.sigmoid(gate_pre)
    activated = gate_pre * sig
    act[...] = activated
    pre[...] = up_pre * (sig * (1.0 + gate_pre * (1.0 - sig)))
    hidden[...] = (activated * up_pre).astype(BF16)
    out = [copies.start(a, b) for a, b in ((act, act_hbm), (pre, pre_hbm), (hidden, hidden_hbm))]
    for copy in out:
        copy.wait()


def hidden_grads(g0, g1, gd, down_hbm, near_hbm, mine_hbm, theirs_hbm, g, down, total, sems):
    copies = Copies(sems)
    units = down.shape[0] // 2
    quarter = g.shape[1] // 2
    eighth = quarter // 2
    parts = (slice(0, eighth), slice(eighth, quarter), slice(quarter, 2 * quarter))
    near, far = piece_order()[:2]
    own = (columns(near, eighth), columns(far, eighth), columns(core(), quarter, 2 * quarter))
    theirs = (columns(side(), eighth), columns(1 - side(), eighth), pl.ds(quarter, quarter))
    got = [
        [
            copies.start(ref, g.at[:, part]),
            copies.start(near_hbm.at[:, a], down.at[:units, part]),
            copies.start(down_hbm.at[0, :, b], down.at[units:, part]),
        ]
        for ref, part, a, b in zip((g0, g1, gd), parts, theirs, own)
    ]
    sums = jnp.zeros(total.shape, F32)
    for copy_list, part in zip(got, parts):
        for copy in copy_list:
            copy.wait()
        sums += dot(down[:, part], g[:, part], NT)
    total[...] = sums
    out = [copies.start(total.at[:units], theirs_hbm), copies.start(total.at[units:], mine_hbm)]
    for copy in out:
        copy.wait()


def cotangents(mine_hbm, got_hbm, act_hbm, pre_hbm, hidden_hbm, pack_hbm, *scratch):
    mine, got, act, pre, hidden, pack, sems = scratch
    copies = Copies(sems)
    units = mine.shape[0]
    pairs = ((mine_hbm, mine), (got_hbm, got), (pre_hbm, pre), (act_hbm, act), (hidden_hbm, hidden))
    started = [copies.start(a, b) for a, b in pairs]
    for copy in started:
        copy.wait()
    hidden_grad = mine[...] + got[...]
    pack[:units] = (hidden_grad * pre[...]).astype(BF16)
    pack[units : 2 * units] = (hidden_grad * act[...]).astype(BF16)
    gate_dot = jnp.sum(hidden[...].astype(F32) * hidden_grad, axis=0, keepdims=True)
    pack[2 * units :] = in_rows(three_parts(gate_dot), TAIL).astype(BF16)
    copies.start(pack, pack_hbm).wait()


def near_row_grad(own_hbm, near_hbm, gate_hbm, up_hbm, both_hbm, out_hbm, *scratch):
    own, near, mine, both, total, sems = scratch
    copies = Copies(sems)
    units, quarter = mine.shape[0] // 2, mine.shape[1]
    at = columns(xlo() * 2 + core(), quarter)
    started = [
        copies.start(own_hbm, own),
        copies.start(gate_hbm.at[0, :, at], mine.at[:units]),
        copies.start(up_hbm.at[0, :, at], mine.at[units:]),
        copies.start(near_hbm, near),
        copies.start(both_hbm, both),
    ]
    for copy in started:
        copy.wait()
    total[...] = dot(own[: 2 * units], mine[...], TN) + dot(near[: 2 * units], both[...], TN)
    copies.start(total, out_hbm).wait()


def row_grad(
    begun_hbm, own_hbm, near_hbm, far_hbm, last_hbm, far_both, last_both, out_hbm, *scratch
):
    total, own, near, far, last, wide, lasting, sent, sems = scratch
    copies = Copies(sems)
    units2, quarter = wide.shape
    pairs = (
        (far_hbm, far),
        (far_both.at[:, columns(core(), quarter)], wide),
        (last_hbm, last),
        (last_both, lasting),
        (begun_hbm, total),
        (own_hbm.at[units2:], own),
        (near_hbm.at[units2:], near),
    )
    started = [copies.start(a, b) for a, b in pairs]
    started[0].wait()
    far_rows = jnp.transpose(far[:units2])
    started[1].wait()
    started[2].wait()
    last_rows = jnp.transpose(last[:units2])
    started[5].wait()
    started[6].wait()
    tails = own[...].astype(F32) + near[...].astype(F32)
    tails += far[units2:].astype(F32) + last[units2:].astype(F32)
    gate_dot = jnp.sum(tails, axis=0, keepdims=True)
    sent[:, quarter:] = jnp.transpose(in_rows(three_parts(gate_dot), LANES)).astype(BF16)
    started[3].wait()
    started[4].wait()
    out = []
    for i in range(2):
        part = slice(i * (quarter // 2), (i + 1) * (quarter // 2))
        sums = dot(far_rows, wide[:, part], NN) + dot(last_rows, lasting[:, part], NN)
        sent[:, part] = (total[:, part] + sums).astype(BF16)
        if i:
            part = slice(quarter // 2, quarter + LANES)
        out.append(copies.start(sent.at[:, part], out_hbm.at[:, part]))
    for copy in out:
        copy.wait()


def weight_grads(pack_hbm, x0, x1, x2, x3, gate_hbm, up_hbm, pack, x, out, sems):
    copies = Copies(sems)
    units, quarter = out.shape[1] // 2, x.shape[2]
    got = [copies.start(pack_hbm.at[: 2 * units], pack)]
    got += [copies.start(ref, x.at[i]) for i, ref in enumerate((x0, x1, x2, x3))]
    got[0].wait()
    sent = []
    for i, at in enumerate(piece_order()):
        got[i + 1].wait()
        out[i] = dot(pack[...], x[i], NN).astype(BF16)
        there = columns(at, quarter)
        sent.append(copies.start(out.at[i, :units], gate_hbm.at[0, :, there]))
        sent.append(copies.start(out.at[i, units:], up_hbm.at[0, :, there]))
    for copy in sent:
        copy.wait()


def weight_grads_down(hidden_hbm, g0, g1, g2, g3, gd0, gd1, down_hbm, *scratch):
    hidden, g, gd, out, direct, sems = scratch
    copies = Copies(sems)
    eighth = g.shape[2]
    got = [copies.start(hidden_hbm, hidden)]
    got += [copies.start(ref, g.at[i]) for i, ref in enumerate((g0, g1, g2, g3))]
    got += [copies.start(ref, gd.at[i]) for i, ref in enumerate((gd0, gd1))]
    got[0].wait()
    sent = []
    for i, at in enumerate(piece_order()):
        got[i + 1].wait()
        out[i] = dot(hidden[...], g[i], NN).astype(BF16)
        sent.append(copies.start(out.at[i], down_hbm.at[0, :, columns(at, eighth)]))
    for i, at in enumerate((core(), 1 - core())):
        got[i + 5].wait()
        direct[i] = dot(hidden[...], gd[i], NN).astype(BF16)
        there = columns(at, 2 * eighth, 4 * eighth)
        sent.append(copies.start(direct.at[i], down_hbm.at[0, :, there]))
    for copy in sent:
        copy.wait()


def combine(first_hbm, second_hbm, back_hbm, gates_hbm, out_hbm, dots_hbm, *scratch):
    first, second, back, gates, out, dots, sems = scratch
    copies = Copies(sems)
    rows, quarter = out.shape
    parts = (slice(0, quarter // 2), slice(quarter // 2, quarter + LANES))
    pairs = ((gates_hbm, gates), (first_hbm, first), (second_hbm, second))
    started = [copies.start(a, b) for a, b in pairs]
    got = [copies.start(back_hbm.at[:, part], back.at[:, part]) for part in parts]
    for copy in started:
        copy.wait()
    weights = jnp.transpose(in_rows((gates[0:1, :], gates[1:2, :]), LANES))
    sent = []
    for i, part in enumerate(parts):
        got[i].wait()
        picked = [dot(ref[...], back[:, part], NN) for ref in (first, second)]
        total = weights[:, 0:1] * picked[0] + weights[:, 1:2] * picked[1]
        there = slice(i * (quarter // 2), (i + 1) * (quarter // 2))
        out[:, there] = total[:, : quarter // 2].astype(BF16)
        sent.append(copies.start(out.at[:, there], out_hbm.at[:, there]))
    lane = lax.broadcasted_iota(jnp.int32, (rows, LANES), 1)
    for i in range(2):
        tail = jnp.transpose(jnp.where(lane < 3, picked[i][:, quarter // 2 :], 0.0))
        dots[i : i + 1, :] = jnp.sum(tail, axis=0, keepdims=True)
    sent.append(copies.start(dots, dots_hbm))
    for copy in sent:
        copy.wait()


def crossing_groups(sizes):
    xhi, z, y = sizes
    groups = []
    for start, one in itertools.product(range(2), range(2)):
        groups.append(
            [
                ((((start ^ h) * 2 + one) * xhi + h) * z + i) * y + j
                for h, i, j in itertools.product(range(xhi), range(z), range(y))
            ]
        )
    return groups


def body(tokens, grads_out, expert_ids, gates, w_gate, w_up, w_down):
    rows, width = tokens.shape
    units = w_gate.shape[1]
    sizes = tuple(lax.axis_size(name) for name in ROWS)
    experts = sizes[0] * sizes[1] * sizes[2]
    slots = experts * CAPACITY
    quarter, half = width // 4, width // 2
    groups = crossing_groups(sizes)

    def exchange(value, axis):
        return lax.ppermute(value, axis, [(0, 1), (1, 0)])

    def to_experts(value):
        shaped = value.reshape(experts, CAPACITY, value.shape[1])
        moved = lax.all_to_all(
            shaped, ALL, split_axis=0, concat_axis=0, tiled=True, axis_index_groups=groups
        )
        return moved.reshape(value.shape)

    def to_tokens(value):
        shaped = value.reshape(experts, CAPACITY, value.shape[1])
        moved = lax.all_to_all(shaped, ROWS, split_axis=0, concat_axis=0, tiled=True)
        return moved.reshape(value.shape)

    unit = 2 * slots * units * quarter
    eighth = width // 8
    ids, gates = expert_ids.T, gates.T
    piece, wide, tall = ((slots, quarter), BF16), ((units, slots), F32), ((2 * units, quarter), BF16)
    pack = ((2 * units + TAIL, slots), BF16)
    hidden_type = ((units, slots), BF16)
    half_down = ((units, half), BF16)
    id_type, chosen = ((2, rows), jnp.int32), ((rows, slots), BF16)

    (sent_first,) = call(
        place_first,
        [((slots, quarter + eighth), BF16)],
        [ids, tokens, grads_out],
        [
            id_type,
            ((rows, quarter), BF16),
            ((rows, eighth), BF16),
            ((slots, quarter + eighth), BF16),
        ],
        6,
        unit // 2,
    )
    got_first = to_experts(sent_first)
    shared = ((2 * units, half), BF16)
    (far_both,) = call(share_far, [shared], [w_gate, w_up], [shared], 4, 1000)
    far_both = exchange(far_both, "xlo")
    near_both, near_down = call(
        share_near, [tall, half_down], [w_gate, w_up, w_down], [tall, half_down], 7, 1000
    )
    near_both, near_down = exchange(near_both, "core"), exchange(near_down, "core")
    (sent_second,) = call(
        place_second,
        [piece],
        [ids, grads_out],
        [id_type, ((rows, quarter), BF16), piece],
        4,
        unit // 2,
    )
    first, second = call(pick, [chosen, chosen], [ids], [id_type, chosen, chosen], 3, unit // 4)
    got_first, first, second, near_both, near_down, far_both = lax.optimization_barrier(
        (got_first, first, second, near_both, near_down, far_both)
    )
    eighth_piece = ((slots, eighth), BF16)
    x0, g0 = call(
        split, [piece, eighth_piece], [got_first], [piece, eighth_piece], 16, 1000, 8 * MIB
    )
    gd0 = to_experts(sent_second)
    x1 = exchange(x0, "xlo")
    x1, g0 = lax.optimization_barrier((x1, g0))
    g1 = exchange(g0, "xlo")
    x2 = exchange(x0, "core")
    x3 = exchange(x1, "core")
    act, pre, hidden = call(
        forward,
        [wide, wide, hidden_type],
        [x0, x1, x2, x3, w_gate, w_up],
        [
            ((4, slots, quarter), BF16),
            ((4, units, quarter), BF16),
            ((4, units, quarter), BF16),
            wide,
            wide,
            hidden_type,
        ],
        15,
        8 * unit,
        63 * MIB,
    )
    act, pre, hidden, gd0, g1 = lax.optimization_barrier((act, pre, hidden, gd0, g1))
    mine, theirs = call(
        hidden_grads,
        [wide, wide],
        [g0, g1, gd0, w_down, near_down],
        [((slots, half), BF16), ((2 * units, half), BF16), ((2 * units, slots), F32)],
        11,
        4 * unit,
    )
    theirs, far_both = lax.optimization_barrier((theirs, far_both))
    got = exchange(theirs, "core")
    (last_both,) = call(pass_on, [tall], [far_both], [tall], 2, 1000)
    last_both = exchange(last_both, "core")
    (own,) = call(
        cotangents,
        [pack],
        [mine, got, act, pre, hidden],
        [wide, wide, wide, wide, hidden_type, pack],
        6,
        10 * slots * units,
        8 * MIB,
    )
    far = exchange(own, "xlo")
    near = exchange(own, "core")
    total = ((slots, quarter), F32)
    (begun,) = call(
        near_row_grad,
        [total],
        [own, near, w_gate, w_up, near_both],
        [pack, pack, tall, tall, total],
        6,
        4 * unit,
    )
    far, begun, g0, g1, gd0, hidden, own = lax.optimization_barrier(
        (far, begun, g0, g1, gd0, hidden, own)
    )
    last = exchange(far, "core")
    tail = ((TAIL, slots), BF16)
    returned = ((slots, quarter + LANES), BF16)
    (sent_r,) = call(
        row_grad,
        [returned],
        [begun, own, near, far, last, far_both, last_both],
        [total, tail, tail, pack, pack, tall, tall, returned],
        9,
        4 * unit,
    )
    sent_r, own, hidden, g0, g1, gd0 = lax.optimization_barrier(
        (sent_r, own, hidden, g0, g1, gd0)
    )
    back = to_tokens(sent_r)
    g2, g3, gd1 = exchange(g0, "core"), exchange(g1, "core"), exchange(gd0, "core")
    grad_gate, grad_up = call(
        weight_grads,
        [(w_gate.shape, BF16), (w_up.shape, BF16)],
        [own, x0, x1, x2, x3],
        [((2 * units, slots), BF16), ((4, slots, quarter), BF16), ((4, 2 * units, quarter), BF16)],
        13,
        8 * unit,
    )
    (grad_down,) = call(
        weight_grads_down,
        [(w_down.shape, BF16)],
        [hidden, g0, g1, g2, g3, gd0, gd1],
        [
            hidden_type,
            ((4, slots, eighth), BF16),
            ((2, slots, quarter), BF16),
            ((4, units, eighth), BF16),
            ((2, units, quarter), BF16),
        ],
        13,
        4 * unit,
    )
    back, grad_gate, grad_up, grad_down = lax.optimization_barrier(
        (back, grad_gate, grad_up, grad_down)
    )
    input_grad, gate_grad = call(
        combine,
        [((rows, quarter), BF16), ((2, rows), F32)],
        [first, second, back, gates],
        [chosen, chosen, returned, ((2, rows), F32), ((rows, quarter), BF16), ((2, rows), F32)],
        8,
        unit,
        8 * MIB,
    )
    return input_grad, gate_grad.T, grad_gate, grad_up, grad_down


def solution(mesh):
    dp, wide, narrow = (mesh.shape[name] for name in ("dp", "wide", "narrow"))
    fine = Mesh(mesh.devices.reshape(2, dp // 2, 2, wide // 2, narrow), ALL)
    by_row, by_part = P(ROWS, None), P(ROWS, PARTS, None)
    return jax.shard_map(
        body,
        mesh=fine,
        in_specs=(by_row, by_row, by_row, by_row, by_part, by_part, by_part),
        out_specs=(P(ROWS, PARTS), by_row, by_part, by_part, by_part),
        check_vma=False,
    )
```
